512 devices in a mesh: span: 8 (over x, core), seq: 64 (over z, y).
Axes of the slice: x: 4, y: 8, z: 8, core: 2. Of those that a mesh axis runs over, the one named last changes fastest.
Arguments:
- latents: bfloat16 [4096, 4096], P(('span', 'seq')), may hold values from -6 to 6
- new_span: bfloat16 [512, 4096], P('seq'), may hold values from -6 to 6
- counts: int32 [9], replicated, may hold values from 128 to 512, as said below
- steps: int32 [2, 8], replicated, may hold values from 0 to 63
- span_mask: int32 [2, 8, 8], replicated, may hold values from 0 to 1, as said below
- q_gain: float32 [64, 4096], replicated, may hold values from -3 to 3
- k_gain: float32 [64, 4096], replicated, may hold values from -3 to 3
- delta: float32 [64], replicated, may hold values from 0.1 to 0.6
Outputs:
- middle: bfloat16 [4096, 4096], P(('span', 'seq'))
- final: bfloat16 [4096, 4096], P(('span', 'seq'))
The draws below stay inside these ranges and needn't reach their ends.
Inputs may be any that keep to these rules, and one draw needn't show every extreme that they name: `counts`: each span has at least a quarter of its 512 slots live, live slots first; some span has all of them live. `span_mask`: each span sees its own keys; a span never sees a later span's keys; earlier spans are seen or not.
All inputs are finite; a program needn't handle non-finite values.
Results may differ from the reference program's by a relative error of at most 0.0083.
Values may be sent and summed in bfloat16 or wider, within the bound.
No kernel may reach another device: no remote copies, remote signals or barrier semaphores. Data moves between devices by JAX's collectives and lax.ppermute only.
A program may use at most 64 MiB of HBM per device.

```python
import math
import jax
import jax.numpy as jnp
from jax import lax

HEADS = 32
HEAD_DIM = 128
NSTEPS = 64
WIDTH = 4096
SPAN = 512
SPANS = 8
N_SPAN = 8


def draw_counts(key, part):
    key = jax.random.fold_in(key, 11)
    values = jax.random.randint(key, (N_SPAN + 1,), SPAN // 4, SPAN + 1)
    place = jax.random.randint(jax.random.fold_in(key, 2), (), 0, N_SPAN + 1)
    spots = jnp.arange(N_SPAN + 1, dtype=jnp.int32)
    return jnp.where(spots == place, SPAN, values).astype(jnp.int32)


def draw_span_mask(key, part):
    key = jax.random.fold_in(key, 23)
    coins = jax.random.randint(key, (2, N_SPAN, N_SPAN), 0, 4)
    rows = jnp.arange(N_SPAN, dtype=jnp.int32)[:, None]
    cols = jnp.arange(N_SPAN, dtype=jnp.int32)[None, :]
    lower = (cols < rows)[None, :, :] & (coins > 0)
    diag = (cols == rows)[None, :, :]
    return jnp.where(diag | lower, 1, 0).astype(jnp.int32)


def with_ends(entries, stream_key, smallest, top_value):
    dims = entries.shape
    index_at = [jax.random.randint(jax.random.fold_in(stream_key, axis), (), 0, dims[axis]) for axis in range(len(dims))]
    entries = entries.at[tuple(index_at)].set(smallest)
    longest = dims.index(max(dims))
    index_at[longest] = (index_at[longest] + 1) % dims[longest]
    return entries.at[tuple(index_at)].set(top_value)


def steps_of(rng, dims, cuts, least, top_value):
    def one(position, shards_of):
        heights = jax.random.uniform(jax.random.fold_in(jax.random.fold_in(rng, 6), position), (shards_of,), jnp.float32, least / len(cuts), top_value / len(cuts))
        return jnp.repeat(jnp.exp(heights), dims[position] // shards_of).reshape((-1,) + (1,) * (len(dims) - position - 1))

    gain = one(*cuts[0])
    for cut in cuts[1:]:
        gain = gain * one(*cut)
    return gain


def noise(key, extent, deviation, most, cuts=(), kind=jnp.bfloat16):
    drawn = jax.random.normal(key, extent, jnp.float32) * deviation
    if len(cuts) > 0:
        drawn = steps_of(key, extent, cuts, -0.22, 0.18) * drawn
    return jnp.clip(drawn, min=-most, max=most).astype(kind)


def setup_inputs(seed: int = 0) -> dict:
    key_of = jax.random.split(jax.random.key(seed), 9)
    return {
        "latents": noise(key_of[0], (SPANS * SPAN, WIDTH), 1.0, 6.0, ((0, 512),)),
        "new_span": noise(key_of[1], (SPAN, WIDTH), 1.0, 6.0, ((0, 64),)),
        "counts": draw_counts(jax.random.fold_in(key_of[8], 71), 0),
        "steps": with_ends(jax.random.randint(key_of[3], (2, SPANS), 0, NSTEPS), jax.random.fold_in(key_of[3], 1), 0, NSTEPS - 1).astype(jnp.int32),
        "span_mask": draw_span_mask(jax.random.fold_in(key_of[8], 71), 0),
        "q_gain": jnp.clip(jax.random.uniform(key_of[5], (NSTEPS, WIDTH), jnp.float32, -3.0, 3.0), -3.0, 3.0),
        "k_gain": jnp.clip(jax.random.uniform(key_of[6], (NSTEPS, WIDTH), jnp.float32, -3.0, 3.0), -3.0, 3.0),
        "delta": jnp.clip(jnp.exp(jax.random.uniform(key_of[7], (NSTEPS,), jnp.float32, math.log(0.1), math.log(0.6))), 0.1, 0.6),
    }


def norm_heads(block):
    rows = block.shape[0]
    parts = block.astype(jnp.float32).reshape(rows, HEADS, HEAD_DIM)
    parts = parts * lax.rsqrt(lax.optimization_barrier(jnp.mean(parts * parts, axis=-1, keepdims=True)) + 1e-06)
    return parts.reshape(rows, HEADS * HEAD_DIM)

def denoise(state, step_ids, counts_now, mask_now, q_gain, k_gain, delta):
    scale = 1.0 / math.sqrt(HEAD_DIM)
    spans = [state[g * SPAN:(g + 1) * SPAN] for g in range(N_SPAN)]
    queries = []
    keys = []
    for g in range(N_SPAN):
        normed = norm_heads(spans[g])
        queries.append((normed * q_gain[step_ids[g]]).astype(jnp.bfloat16))
        keys.append((normed * k_gain[step_ids[g]]).astype(jnp.bfloat16))
    slots = jnp.arange(SPAN, dtype=jnp.int32)
    results = []
    for g in range(N_SPAN):
        key_rows = jnp.concatenate(keys[:g + 1], axis=0)
        val_rows = state[:(g + 1) * SPAN]
        live = jnp.concatenate([(slots < counts_now[j]) & (mask_now[g, j] > 0) for j in range(g + 1)])
        q_heads = queries[g].reshape(SPAN, HEADS, HEAD_DIM).transpose(1, 0, 2)
        k_heads = key_rows.reshape(-1, HEADS, HEAD_DIM).transpose(1, 0, 2)
        v_heads = val_rows.reshape(-1, HEADS, HEAD_DIM).transpose(1, 0, 2)

        def one_head(items):
            qa, ka, va = items
            score = jnp.dot(qa, ka.T, preferred_element_type=jnp.float32) * scale
            score = jnp.where(live[None, :], score, -jnp.inf)
            top = lax.optimization_barrier(jnp.max(score, axis=-1, keepdims=True))
            weight = jnp.exp(score - top)
            total = lax.optimization_barrier(jnp.sum(weight, axis=-1, keepdims=True))
            summed = jnp.dot(weight.astype(jnp.bfloat16), va, preferred_element_type=jnp.float32)
            return (summed / total).astype(jnp.bfloat16)
        attended = lax.map(one_head, (q_heads, k_heads, v_heads))
        attended = attended.transpose(1, 0, 2).reshape(SPAN, HEADS * HEAD_DIM)
        rate = delta[step_ids[g]]
        old = spans[g].astype(jnp.float32)
        results.append((old + rate * (attended.astype(jnp.float32) - old)).astype(jnp.bfloat16))
    return jnp.concatenate(results, axis=0)

def reference(latents, new_span, counts, steps, span_mask, q_gain, k_gain, delta):
    middle = denoise(latents, steps[0], counts[:N_SPAN], span_mask[0], q_gain, k_gain, delta)
    entering = jnp.concatenate([middle[SPAN:], new_span], axis=0)
    final = denoise(entering, steps[1], counts[1:], span_mask[1], q_gain, k_gain, delta)
    return (middle, final)
```

```python
import functools
import math

import jax
import jax.numpy as jnp
from jax import lax
from jax.experimental import pallas as pl
from jax.experimental.pallas import tpu as pltpu
from jax.sharding import Mesh
from jax.sharding import PartitionSpec as P

HEAD_DIM = 128
SPAN = 512
SPANS = 8
HALF = SPAN // 2
SCORE_SCALE = math.log2(math.e) / math.sqrt(HEAD_DIM)
SHIFT = 40.0
SMALL = 2.0**-60


def normed(x):
    x = x.astype(jnp.float32)
    return x * lax.rsqrt(jnp.mean(x * x, axis=-1, keepdims=True) + 1e-06)


def head_kernel(
    place,
    counts,
    steps,
    mask,
    delta,
    q_gain,
    k_gain,
    same,
    other,
    fresh,
    out,
    qg,
    kg,
    xs,
    query,
    key,
    value,
    query2,
    key2,
    value2,
    acc,
    low,
    sems,
):
    g, half, head, core = place()
    cols = pl.ds(pl.multiple_of(head * HEAD_DIM, HEAD_DIM), HEAD_DIM)
    copies = [
        pltpu.make_async_copy(q_gain.at[:, cols], qg, sems.at[0]),
        pltpu.make_async_copy(k_gain.at[:, cols], kg, sems.at[1]),
    ]
    for copy in copies:
        copy.start()
    for copy in copies:
        copy.wait()

    slot = lax.broadcasted_iota(jnp.int32, (SPAN, HEAD_DIM), 0)

    def make_key(x, t, live, i, key, value):
        n = normed(x)
        key[i] = (n * kg[pl.ds(t, 1), :]).T.astype(jnp.bfloat16)
        alive = slot < live
        value[i, :, :HEAD_DIM] = jnp.where(alive, x.astype(jnp.float32), 0.0).astype(jnp.bfloat16)
        value[i, :, HEAD_DIM:] = jnp.where(alive, 1.0, 0.0).astype(jnp.bfloat16)
        return n

    def make_query(n, t):
        return (n * qg[pl.ds(t, 1), :]).astype(jnp.bfloat16)

    last = jnp.minimum(g + half, SPANS - 1)
    for a in range(SPANS // 2):
        for source, j in ((same, 2 * a + core), (other, 2 * a + 1 - core)):

            @pl.when(j <= last)
            def _():
                x = source[a]
                xs[j] = x
                t = steps[0, j]
                n = make_key(x, t, counts[j], j, key, value)
                query[j] = make_query(n, t)

    def attend(q, rows, key, value, row_mask, live, upto, safe):
        acc[:rows] = jnp.zeros((rows, 2 * HEAD_DIM), jnp.float32)
        if safe:
            low[:rows] = jnp.full((rows, HEAD_DIM), -1e30, jnp.float32)

        def scores(i, width):
            s = jnp.dot(q, key[i, :, :width], preferred_element_type=jnp.float32) * SCORE_SCALE
            if not safe:
                return s
            at = lax.broadcasted_iota(jnp.int32, (rows, width), 1)
            return jnp.where(at < live(i), s, -1e30)

        def over_spans(step):
            def one(i, carry):
                @pl.when(row_mask(i) > 0)
                def _():
                    @pl.when(live(i) > HALF)
                    def _():
                        step(i, SPAN)

                    @pl.when(live(i) <= HALF)
                    def _():
                        step(i, HALF)

                return carry

            lax.fori_loop(0, upto, one, 0)

        def highest(i, width):
            top = jnp.max(scores(i, width), axis=-1, keepdims=True)
            low[:rows] = jnp.maximum(low[:rows], top)

        def add(i, width):
            shift = low[:rows, :1] if safe else SHIFT
            weight = jnp.exp2(scores(i, width) - shift).astype(jnp.bfloat16)
            acc[:rows] += jnp.dot(weight, value[i, :width], preferred_element_type=jnp.float32)

        if safe:
            over_spans(highest)
        over_spans(add)

    def finish(x, rows, rate):
        total = acc[:rows, HEAD_DIM:]
        attended = (acc[:rows, :HEAD_DIM] / total).astype(jnp.bfloat16).astype(jnp.float32)
        old = x.astype(jnp.float32)
        return (old + rate * (attended - old)).astype(jnp.bfloat16), jnp.min(total)

    def first_step(safe):
        def one(j, worst):
            whole = jnp.logical_or(half == 0, j == g + 1)
            needed = jnp.where(half == 0, j == g, jnp.logical_and(j >= 1, mask[1, g, jnp.maximum(j - 1, 0)] > 0))
            t = steps[0, j]
            live = lambda i: counts[i]

            def block(rows):
                attend(query[j, :rows], rows, key, value, lambda i: mask[0, j, i], live, j + 1, safe)
                x, least = finish(xs[j, :rows], rows, delta[t])

                @pl.when(half == 0)
                def _():
                    out[:rows] = x

                @pl.when(half == 1)
                def _():
                    e = j - 1
                    n = normed(x)
                    t2 = steps[1, e]
                    key2[e, :, :rows] = (n * kg[pl.ds(t2, 1), :]).T.astype(jnp.bfloat16)
                    alive = slot[:rows] < counts[j]
                    value2[e, :rows, :HEAD_DIM] = jnp.where(alive, x.astype(jnp.float32), 0.0).astype(jnp.bfloat16)
                    value2[e, :rows, HEAD_DIM:] = jnp.where(alive, 1.0, 0.0).astype(jnp.bfloat16)

                    @pl.when(e == g)
                    def _():
                        xs[SPANS, :rows] = x
                        query2[:rows] = make_query(n, t2)

                return least

            def run():
                return lax.cond(
                    jnp.logical_or(whole, counts[j] > HALF), lambda: block(SPAN), lambda: block(HALF)
                )

            return jnp.minimum(worst, lax.cond(needed, run, lambda: jnp.float32(1.0)))

        return lax.fori_loop(0, last + 1, one, jnp.float32(1.0))

    @pl.when(first_step(False) < SMALL)
    def _():
        first_step(True)

    def second_step(safe):
        attend(query2[...], SPAN, key2, value2, lambda e: mask[1, g, e], lambda e: counts[e + 1], g + 1, safe)
        x, least = finish(xs[SPANS], SPAN, delta[steps[1, g]])
        out[...] = x
        return least

    @pl.when(half == 1)
    def _():
        @pl.when(g == SPANS - 1)
        def _():
            x = fresh[...]
            xs[SPANS] = x
            t2 = steps[1, g]
            n = make_key(x, t2, counts[SPANS], SPANS - 1, key2, value2)
            query2[...] = make_query(n, t2)

        @pl.when(second_step(False) < SMALL)
        def _():
            second_step(True)


def mesh_place():
    seq = lax.axis_index("seq")
    core = lax.axis_index("core")
    return 2 * lax.axis_index("x") + core, lax.rem(seq, 2), seq // 2, core


def both_steps(place, counts, steps, mask, delta, q_gain, k_gain, same, other, fresh, interpret=False):
    smem = pl.BlockSpec(memory_space=pltpu.SMEM)
    hbm = pl.BlockSpec(memory_space=pl.ANY)
    vmem = pl.BlockSpec(memory_space=pltpu.VMEM)
    noise_steps = q_gain.shape[0]
    bf16, f32 = jnp.bfloat16, jnp.float32
    return pl.pallas_call(
        functools.partial(head_kernel, place),
        out_shape=jax.ShapeDtypeStruct((SPAN, HEAD_DIM), bf16),
        in_specs=[smem, smem, smem, smem, hbm, hbm, vmem, vmem, vmem],
        out_specs=vmem,
        scratch_shapes=[
            pltpu.VMEM((noise_steps, HEAD_DIM), f32),
            pltpu.VMEM((noise_steps, HEAD_DIM), f32),
            pltpu.VMEM((SPANS + 1, SPAN, HEAD_DIM), bf16),
            pltpu.VMEM((SPANS, SPAN, HEAD_DIM), bf16),
            pltpu.VMEM((SPANS, HEAD_DIM, SPAN), bf16),
            pltpu.VMEM((SPANS, SPAN, 2 * HEAD_DIM), bf16),
            pltpu.VMEM((SPAN, HEAD_DIM), bf16),
            pltpu.VMEM((SPANS, HEAD_DIM, SPAN), bf16),
            pltpu.VMEM((SPANS, SPAN, 2 * HEAD_DIM), bf16),
            pltpu.VMEM((SPAN, 2 * HEAD_DIM), f32),
            pltpu.VMEM((SPAN, HEAD_DIM), f32),
            pltpu.SemaphoreType.DMA((2,)),
        ],
        compiler_params=pltpu.CompilerParams(vmem_limit_bytes=32 * 1024 * 1024),
        interpret=interpret,
    )(counts, steps, mask, delta, q_gain, k_gain, same, other, fresh)


def per_device(latents, new_span, counts, steps, span_mask, q_gain, k_gain, delta):
    rows, width = latents.shape
    heads = width // HEAD_DIM

    def to_heads(block):
        return block.reshape(rows, heads, HEAD_DIM).transpose(1, 0, 2)

    sent = jnp.concatenate([to_heads(latents), to_heads(new_span)], axis=1)
    sent = jnp.broadcast_to(sent[:, None], (heads, 2, 2 * rows, HEAD_DIM)).reshape(2 * heads, 2 * rows, HEAD_DIM)
    got = lax.all_to_all(sent, "seq", 0, 0, tiled=True)
    mine = got[:, :rows].reshape(SPAN, HEAD_DIM)
    fresh = got[:, rows:].reshape(SPAN, HEAD_DIM)
    same = lax.all_gather(mine, "x", axis=0)
    other = lax.ppermute(same, "core", [(0, 1), (1, 0)])
    done = both_steps(mesh_place, counts, steps, span_mask, delta, q_gain, k_gain, same, other, fresh)
    back = lax.all_to_all(done.reshape(2 * heads, rows, HEAD_DIM), "seq", 0, 0, tiled=True)
    back = back.reshape(heads, 2, rows, HEAD_DIM)
    return tuple(back[:, k].transpose(1, 0, 2).reshape(rows, width) for k in range(2))


def solution(mesh):
    mesh = Mesh(mesh.devices.reshape(4, 2, 64), ("x", "core", "seq"))
    tokens = P(("x", "core", "seq"), None)
    in_specs = (tokens, P("seq", None), P(), P(), P(), P(), P(), P())
    return jax.shard_map(per_device, mesh=mesh, in_specs=in_specs, out_specs=(tokens, tokens), check_vma=False)
```

```python
import functools
import math

import jax
import jax.numpy as jnp
from jax import lax
from jax.experimental import pallas as pl
from jax.experimental.pallas import tpu as pltpu
from jax.sharding import Mesh
from jax.sharding import PartitionSpec as P

HEAD_DIM = 128
SPAN = 512
SPANS = 8
KEYS = 128
PER_SPAN = SPAN // KEYS
NONE = SPANS * PER_SPAN
GROUP = 4
ENTERING, MIDDLE, UNUSED = SPANS, SPANS + 1, SPANS + 2
SCORE_SCALE = math.log2(math.e) / math.sqrt(HEAD_DIM)
SHIFT = 40.0
SMALL = 2.0**-60


def normed(x):
    x = x.astype(jnp.float32)
    return x * lax.rsqrt(jnp.mean(x * x, axis=-1, keepdims=True) + 1e-06)


def head_kernel(
    place,
    counts,
    steps,
    mask,
    delta,
    q_gain,
    k_gain,
    same,
    other,
    fresh,
    out,
    qg,
    kg,
    xs,
    query,
    key,
    value,
    query2,
    key2,
    value2,
    acc,
    top,
    least,
    blocks,
    todo,
    shares,
    sems,
):
    g, half, head, core = place()
    cols = pl.ds(pl.multiple_of(head * HEAD_DIM, HEAD_DIM), HEAD_DIM)
    copies = [
        pltpu.make_async_copy(q_gain.at[:, cols], qg, sems.at[0]),
        pltpu.make_async_copy(k_gain.at[:, cols], kg, sems.at[1]),
    ]
    for copy in copies:
        copy.start()
    for keys, values in ((key, value), (key2, value2)):
        keys[NONE] = jnp.zeros((HEAD_DIM, KEYS), jnp.bfloat16)
        values[NONE] = jnp.zeros((KEYS, 2 * HEAD_DIM), jnp.bfloat16)

    def put_values(x, live, i, values):
        alive = lax.broadcasted_iota(jnp.int32, (SPAN, HEAD_DIM), 0) < live
        kept = jnp.where(alive, x.astype(jnp.float32), 0.0).astype(jnp.bfloat16)
        ones = jnp.where(alive, 1.0, 0.0).astype(jnp.bfloat16)
        for r in range(PER_SPAN):
            values[PER_SPAN * i + r, :, :HEAD_DIM] = kept[r * KEYS : (r + 1) * KEYS]
            values[PER_SPAN * i + r, :, HEAD_DIM:] = ones[r * KEYS : (r + 1) * KEYS]

    def put_keys(n, t, i, keys):
        turned = (n * kg[pl.ds(t, 1), :]).astype(jnp.bfloat16).T
        for r in range(PER_SPAN):
            keys[PER_SPAN * i + r] = turned[:, r * KEYS : (r + 1) * KEYS]

    def make_query(n, t):
        return (n * qg[pl.ds(t, 1), :]).astype(jnp.bfloat16)

    last = jnp.minimum(g + 1, SPANS - 1)

    def each_pair(step):
        for a in range(SPANS // 2):

            @pl.when(2 * a <= last)
            def _():
                for source, j in ((same, 2 * a + core), (other, 2 * a + 1 - core)):
                    step(source[a], j)

    def values_of(x, j):
        xs[j] = x
        put_values(x, counts[j], j, value)

    def keys_of(x, j):
        t = steps[0, j]
        n = normed(x)
        put_keys(n, t, j, key)
        query[j] = make_query(n, t)

    each_pair(values_of)
    for copy in copies:
        copy.wait()
    each_pair(keys_of)

    def list_blocks(seen, live):
        size = jnp.int32(0)
        for i in range(SPANS):
            for r in range(PER_SPAN):
                blocks[size + r] = PER_SPAN * i + r
            size += jnp.where(seen(i) > 0, (live(i) + KEYS - 1) // KEYS, 0)
        for r in range(2 * GROUP):
            blocks[size + r] = NONE
        return size

    def group(q, keys, values, first, pairs):
        weights, parts = [], []
        for r in range(pairs):
            left, right = blocks[first + 2 * r], blocks[first + 2 * r + 1]
            score = jnp.dot(
                q, jnp.concatenate([keys[left], keys[right]], axis=1), preferred_element_type=jnp.float32
            )
            weights.append(jnp.exp2(score * SCORE_SCALE - SHIFT).astype(jnp.bfloat16))
        for r in range(pairs):
            left, right = blocks[first + 2 * r], blocks[first + 2 * r + 1]
            parts.append(
                jnp.dot(
                    weights[r],
                    jnp.concatenate([values[left], values[right]], axis=0),
                    preferred_element_type=jnp.float32,
                )
            )
        return sum(parts[1:], parts[0])

    def attend(q, rows, keys, values, size, slot):
        acc[slot, :rows] = group(q, keys, values, 0, GROUP)
        if rows < SPAN:
            acc[slot, rows:] = jnp.ones((SPAN - rows, 2 * HEAD_DIM), jnp.float32)
        rest = jnp.maximum((size + 1) // 2 - GROUP, 0)
        whole = (rest + 1) // GROUP

        def more(n, carry):
            acc[slot, :rows] += group(q, keys, values, 2 * GROUP * (n + 1), GROUP)
            return carry

        lax.fori_loop(0, whole, more, 0)

        @pl.when(rest > GROUP * whole)
        def _():
            acc[slot, :rows] += group(q, keys, values, 2 * GROUP * (whole + 1), GROUP // 2)

    def attend_safe(q, keys, values, size, live, slot):
        def scores(b):
            score = jnp.dot(q, keys[b], preferred_element_type=jnp.float32) * SCORE_SCALE
            at = lax.broadcasted_iota(jnp.int32, (SPAN, KEYS), 1) + lax.rem(b, PER_SPAN) * KEYS
            return jnp.where(at < live(b // PER_SPAN), score, -1e30)

        def highest(n, carry):
            top[...] = jnp.maximum(top[...], jnp.max(scores(blocks[n]), axis=-1, keepdims=True))
            return carry

        def add(n, carry):
            weight = jnp.exp2(scores(blocks[n]) - top[...]).astype(jnp.bfloat16)
            acc[slot] += jnp.dot(weight, values[blocks[n]], preferred_element_type=jnp.float32)
            return carry

        top[...] = jnp.full((SPAN, KEYS), -1e30, jnp.float32)
        acc[slot] = jnp.zeros((SPAN, 2 * HEAD_DIM), jnp.float32)
        lax.fori_loop(0, size, highest, 0)
        lax.fori_loop(0, size, add, 0)

    def attended(slot):
        total = acc[slot, :, HEAD_DIM:]
        return acc[slot, :, :HEAD_DIM] / jnp.where(total > 0.0, total, 1.0), total

    def moved(x, target, rate):
        old = x.astype(jnp.float32)
        return old + rate * (target - old)

    def enter(j, slot, counted=True):
        target, total = attended(slot)
        smallest = jnp.min(total.reshape(SPAN // 8, 8, HEAD_DIM), axis=0)
        least[...] = jnp.minimum(least[...], jnp.where(counted, smallest, 1.0))
        target = target.astype(jnp.bfloat16).astype(jnp.float32)
        x = moved(xs[j], target, delta[steps[0, j]]).astype(jnp.bfloat16)
        e = jnp.maximum(j - 1, 0)
        t = steps[1, e]
        n = normed(x)
        put_values(x, counts[j], e, value2)
        put_keys(n, t, e, key2)
        xs[jnp.where(j == g + 1, ENTERING, jnp.where(j == g, MIDDLE, UNUSED))] = x
        query2[jnp.where(j == g + 1, 0, 1)] = make_query(n, t)

    def blocks_of(j):
        return list_blocks(lambda i: mask[0, j, i], lambda i: counts[i])

    lives = [(counts[i] + KEYS - 1) // KEYS for i in range(SPANS + 1)]
    todo[0] = g + 1
    wanted = jnp.where(g < SPANS - 1, 1, 0)
    loads = [jnp.int32(0), PER_SPAN * counts[jnp.minimum(g + 1, SPANS)] // KEYS]
    shares[SPANS - 1] = jnp.where(jnp.logical_and(half == 1, g == SPANS - 1), 1, 0)
    for j in reversed(range(SPANS)):
        own = j == g
        read = jnp.logical_and(j <= g, mask[1, g, j - 1] > 0) if j > 0 else jnp.bool_(False)
        cost = sum(jnp.where(mask[0, j, i] > 0, lives[i], 0) for i in range(j + 1))
        cost = jnp.where(own, PER_SPAN, lives[j]) * cost + PER_SPAN * lives[j] + PER_SPAN
        maker = jnp.where(jnp.logical_or(own, loads[0] <= loads[1]), 0, 1)
        made = jnp.logical_or(own, read)
        for k in range(2):
            loads[k] += jnp.where(jnp.logical_and(made, maker == k), cost, 0)
        mine = jnp.logical_and(made, maker == half)
        todo[wanted] = j
        wanted += jnp.where(mine, 1, 0)
        if j > 0:
            last_one = jnp.logical_and(half == 1, j - 1 == g)
            shares[j - 1] = jnp.where(jnp.logical_or(jnp.logical_and(mine, read), last_one), 1, 0)

    least[...] = jnp.ones((8, HEAD_DIM), jnp.float32)

    def one(m, carry):
        j, before = todo[m], todo[jnp.maximum(m - 1, 0)]
        size = blocks_of(j)
        slot = lax.rem(m, 2)

        def block(rows):
            enter(before, 1 - slot, m > 0)
            attend(query[j, :rows], rows, key, value, size, slot)

        rows = jnp.where(jnp.logical_or(j == g + 1, j == g), SPAN, counts[j])
        for r in range(2, PER_SPAN + 1):
            fits = rows <= r * KEYS
            if r > 2:
                fits = jnp.logical_and(fits, rows > (r - 1) * KEYS)
            pl.when(fits)(functools.partial(block, r * KEYS))
        return carry

    lax.fori_loop(0, wanted, one, 0)

    @pl.when(wanted > 0)
    def _():
        enter(todo[wanted - 1], lax.rem(wanted - 1, 2))

    @pl.when(jnp.min(least[...]) < SMALL)
    def _():
        def one_safe(m, carry):
            j = todo[m]
            attend_safe(query[j], key, value, blocks_of(j), lambda i: counts[i], 0)
            enter(j, 0)
            return carry

        lax.fori_loop(0, wanted, one_safe, 0)

    @pl.when(g == SPANS - 1)
    def _():
        x = fresh[...]
        xs[ENTERING] = x
        t = steps[1, g]
        n = normed(x)
        put_values(x, counts[SPANS], SPANS - 1, value2)
        put_keys(n, t, SPANS - 1, key2)
        query2[0] = make_query(n, t)

    size = list_blocks(lambda e: shares[e], lambda e: counts[e + 1])
    rate = delta[steps[1, g]]

    def put(row, x):
        out[:, row : row + 8] = x.reshape(SPAN // 8, 8, HEAD_DIM).astype(jnp.bfloat16)

    def put_final(scale):
        target, total = attended(0)
        put(8, moved(xs[ENTERING], target, rate))
        put(16, jnp.where(total > 0.0, jnp.sqrt(total) * scale, 0.0))
        return jnp.min(total)

    put(0, xs[MIDDLE].astype(jnp.float32))
    attend(query2[0], SPAN, key2, value2, size, 0)

    @pl.when(jnp.logical_and(put_final(2.0 ** (SHIFT / 2)) < SMALL, size > 0))
    def _():
        attend_safe(query2[0], key2, value2, size, lambda e: counts[e + 1], 0)
        put_final(jnp.exp2(top[...] * 0.5))


def mesh_place():
    seq = lax.axis_index("seq")
    core = lax.axis_index("core")
    return 2 * lax.axis_index("x") + core, lax.rem(seq, 2), seq // 2, core


def both_steps(place, counts, steps, mask, delta, q_gain, k_gain, same, other, fresh, interpret=False):
    smem = pl.BlockSpec(memory_space=pltpu.SMEM)
    hbm = pl.BlockSpec(memory_space=pl.ANY)
    vmem = pl.BlockSpec(memory_space=pltpu.VMEM)
    noise_steps = q_gain.shape[0]
    bf16, f32 = jnp.bfloat16, jnp.float32
    return pl.pallas_call(
        functools.partial(head_kernel, place),
        out_shape=jax.ShapeDtypeStruct((SPAN // 8, 24, HEAD_DIM), bf16),
        in_specs=[smem, smem, smem, smem, hbm, hbm, vmem, vmem, vmem],
        out_specs=vmem,
        scratch_shapes=[
            pltpu.VMEM((noise_steps, HEAD_DIM), f32),
            pltpu.VMEM((noise_steps, HEAD_DIM), f32),
            pltpu.VMEM((UNUSED + 1, SPAN, HEAD_DIM), bf16),
            pltpu.VMEM((SPANS, SPAN, HEAD_DIM), bf16),
            pltpu.VMEM((NONE + 1, HEAD_DIM, KEYS), bf16),
            pltpu.VMEM((NONE + 1, KEYS, 2 * HEAD_DIM), bf16),
            pltpu.VMEM((2, SPAN, HEAD_DIM), bf16),
            pltpu.VMEM((NONE + 1, HEAD_DIM, KEYS), bf16),
            pltpu.VMEM((NONE + 1, KEYS, 2 * HEAD_DIM), bf16),
            pltpu.VMEM((2, SPAN, 2 * HEAD_DIM), f32),
            pltpu.VMEM((SPAN, KEYS), f32),
            pltpu.VMEM((8, HEAD_DIM), f32),
            pltpu.SMEM((NONE + 2 * GROUP,), jnp.int32),
            pltpu.SMEM((SPANS + 2,), jnp.int32),
            pltpu.SMEM((SPANS,), jnp.int32),
            pltpu.SemaphoreType.DMA((2,)),
        ],
        compiler_params=pltpu.CompilerParams(vmem_limit_bytes=32 * 1024 * 1024),
        interpret=interpret,
    )(counts, steps, mask, delta, q_gain, k_gain, same, other, fresh)


def per_device(latents, new_span, counts, steps, span_mask, q_gain, k_gain, delta):
    rows, width = latents.shape
    heads = width // HEAD_DIM

    def to_heads(block):
        return block.reshape(rows, heads, HEAD_DIM).transpose(1, 0, 2)

    sent = jnp.concatenate([to_heads(latents), to_heads(new_span)], axis=1)
    sent = jnp.broadcast_to(sent[:, None], (heads, 2, 2 * rows, HEAD_DIM)).reshape(2 * heads, 2 * rows, HEAD_DIM)
    got = lax.all_to_all(sent, "seq", 0, 0, tiled=True)
    mine = got[:, :rows].reshape(SPAN, HEAD_DIM)
    fresh = got[:, rows:].reshape(SPAN, HEAD_DIM)
    same = lax.all_gather(mine, "x", axis=0)
    other = lax.ppermute(same, "core", [(0, 1), (1, 0)])
    done = both_steps(mesh_place, counts, steps, span_mask, delta, q_gain, k_gain, same, other, fresh)
    back = lax.all_to_all(done, "seq", 0, 0, tiled=True)
    back = back.reshape(heads, 2, 3 * rows, HEAD_DIM)

    def to_tokens(block):
        return block.transpose(1, 0, 2).reshape(rows, width)

    part = back[:, :, rows : 2 * rows].astype(jnp.float32)
    root = back[:, :, 2 * rows :].astype(jnp.float32)
    ratio = root[:, 0] / root[:, 1]
    share = 1.0 / (1.0 + ratio * ratio)
    final = part[:, 0] + share * (part[:, 1] - part[:, 0])
    return to_tokens(back[:, 0, :rows]), to_tokens(final.astype(jnp.bfloat16))


def solution(mesh):
    mesh = Mesh(mesh.devices.reshape(4, 2, 64), ("x", "core", "seq"))
    tokens = P(("x", "core", "seq"), None)
    in_specs = (tokens, P("seq", None), P(), P(), P(), P(), P(), P())
    return jax.shard_map(per_device, mesh=mesh, in_specs=in_specs, out_specs=(tokens, tokens), check_vma=False)
```

```python
import functools
import math

import jax
import jax.numpy as jnp
from jax import lax
from jax.experimental import pallas as pl
from jax.experimental.pallas import tpu as pltpu
from jax.sharding import Mesh
from jax.sharding import PartitionSpec as P

HEAD_DIM = 128
SPAN = 512
SPANS = 8
HALF = SPAN // 2
KEYS = 128
PER_SPAN = SPAN // KEYS
NONE = SPANS * PER_SPAN
GROUP = 4
ENTERING, MIDDLE, UNUSED = 0, 1, 2
SCORE_SCALE = math.log2(math.e) / math.sqrt(HEAD_DIM)
SHIFT = 40.0
SMALL = 2.0**-60


def normed(x):
    x = x.astype(jnp.float32)
    return x * lax.rsqrt(jnp.mean(x * x, axis=-1, keepdims=True) + 1e-06)


def head_kernel(
    place,
    counts,
    steps,
    mask,
    delta,
    q_gain,
    k_gain,
    same,
    other,
    fresh,
    out,
    qg,
    kg,
    xs,
    query,
    key,
    value,
    query2,
    key2,
    value2,
    acc,
    top,
    least,
    blocks,
    todo,
    sent,
    sems,
):
    g, half, head, core = place()
    cols = pl.ds(pl.multiple_of(head * HEAD_DIM, HEAD_DIM), HEAD_DIM)
    copies = [
        pltpu.make_async_copy(q_gain.at[:, cols], qg, sems.at[0]),
        pltpu.make_async_copy(k_gain.at[:, cols], kg, sems.at[1]),
    ]
    for copy in copies:
        copy.start()
    for keys, values in ((key, value), (key2, value2)):
        keys[NONE] = jnp.zeros((HEAD_DIM, KEYS), jnp.bfloat16)
        values[NONE] = jnp.zeros((KEYS, 2 * HEAD_DIM), jnp.bfloat16)

    def put_values(x, live, i, values):
        alive = lax.broadcasted_iota(jnp.int32, (SPAN, HEAD_DIM), 0) < live
        kept = jnp.where(alive, x.astype(jnp.float32), 0.0).astype(jnp.bfloat16)
        ones = jnp.where(alive, 1.0, 0.0).astype(jnp.bfloat16)
        for r in range(PER_SPAN):
            values[PER_SPAN * i + r, :, :HEAD_DIM] = kept[r * KEYS : (r + 1) * KEYS]
            values[PER_SPAN * i + r, :, HEAD_DIM:] = ones[r * KEYS : (r + 1) * KEYS]

    def put_keys(n, t, i, keys):
        turned = (n * kg[pl.ds(t, 1), :]).astype(jnp.bfloat16).T
        for r in range(PER_SPAN):
            keys[PER_SPAN * i + r] = turned[:, r * KEYS : (r + 1) * KEYS]

    def make_query(n, t):
        return (n * qg[pl.ds(t, 1), :]).astype(jnp.bfloat16)

    last = jnp.minimum(g + 1, SPANS - 1)

    def each_pair(step):
        for a in range(SPANS // 2):

            @pl.when(2 * a <= last)
            def _():
                for source, j in ((same, 2 * a + core), (other, 2 * a + 1 - core)):
                    step(source[a], j)

    def values_of(x, j):
        xs[j] = x
        put_values(x, counts[j], j, value)

    def keys_of(x, j):
        t = steps[0, j]
        n = normed(x)
        put_keys(n, t, j, key)
        query[j] = make_query(n, t)

    each_pair(values_of)
    for copy in copies:
        copy.wait()
    each_pair(keys_of)

    def list_blocks(seen, live):
        size = jnp.int32(0)
        for i in range(SPANS):
            for r in range(PER_SPAN):
                blocks[size + r] = PER_SPAN * i + r
            size += jnp.where(seen(i) > 0, (live(i) + KEYS - 1) // KEYS, 0)
        for r in range(2 * GROUP):
            blocks[size + r] = NONE
        return size

    def group(q, keys, values, first, pairs):
        weights, parts = [], []
        for r in range(pairs):
            left, right = blocks[first + 2 * r], blocks[first + 2 * r + 1]
            score = jnp.dot(
                q, jnp.concatenate([keys[left], keys[right]], axis=1), preferred_element_type=jnp.float32
            )
            weights.append(jnp.exp2(score * SCORE_SCALE - SHIFT).astype(jnp.bfloat16))
        for r in range(pairs):
            left, right = blocks[first + 2 * r], blocks[first + 2 * r + 1]
            parts.append(
                jnp.dot(
                    weights[r],
                    jnp.concatenate([values[left], values[right]], axis=0),
                    preferred_element_type=jnp.float32,
                )
            )
        return sum(parts[1:], parts[0])

    def attend(q, rows, keys, values, size, slot):
        acc[slot, :rows] = group(q, keys, values, 0, GROUP)
        if rows < SPAN:
            acc[slot, rows:] = jnp.ones((SPAN - rows, 2 * HEAD_DIM), jnp.float32)
        rest = jnp.maximum((size + 1) // 2 - GROUP, 0)
        whole = (rest + 1) // GROUP

        def more(n, carry):
            acc[slot, :rows] += group(q, keys, values, 2 * GROUP * (n + 1), GROUP)
            return carry

        lax.fori_loop(0, whole, more, 0)

        @pl.when(rest > GROUP * whole)
        def _():
            acc[slot, :rows] += group(q, keys, values, 2 * GROUP * (whole + 1), GROUP // 2)

    def attend_safe(q, rows, keys, values, size, live, slot):
        def scores(b):
            score = jnp.dot(q, keys[b], preferred_element_type=jnp.float32) * SCORE_SCALE
            at = lax.broadcasted_iota(jnp.int32, (rows, KEYS), 1) + lax.rem(b, PER_SPAN) * KEYS
            return jnp.where(at < live(b // PER_SPAN), score, -1e30)

        def highest(n, carry):
            top[:rows] = jnp.maximum(top[:rows], jnp.max(scores(blocks[n]), axis=-1, keepdims=True))
            return carry

        def add(n, carry):
            weight = jnp.exp2(scores(blocks[n]) - top[:rows]).astype(jnp.bfloat16)
            acc[slot, :rows] += jnp.dot(weight, values[blocks[n]], preferred_element_type=jnp.float32)
            return carry

        top[:rows] = jnp.full((rows, KEYS), -1e30, jnp.float32)
        acc[slot, :rows] = jnp.zeros((rows, 2 * HEAD_DIM), jnp.float32)
        lax.fori_loop(0, size, highest, 0)
        lax.fori_loop(0, size, add, 0)

    def finish(x, rows, slot, rate):
        total = acc[slot, :rows, HEAD_DIM:]
        target = (acc[slot, :rows, :HEAD_DIM] / total).astype(jnp.bfloat16).astype(jnp.float32)
        old = x.astype(jnp.float32)
        return (old + rate * (target - old)).astype(jnp.bfloat16), total

    def sent_rows(x):
        pieces = x.astype(jnp.float32).reshape(SPAN // 16, 2, 8, HEAD_DIM)
        return jnp.where(half == 0, pieces[:, 0], pieces[:, 1])

    def enter(j, slot, counted=True):
        x, total = finish(xs[j], SPAN, slot, delta[steps[0, j]])
        smallest = jnp.min(total.reshape(SPAN // 8, 8, HEAD_DIM), axis=0)
        least[...] = jnp.minimum(least[...], jnp.where(counted, smallest, 1.0))
        e = jnp.where(j > 0, j - 1, SPANS - 1)
        t = steps[1, e]
        n = normed(x)
        put_values(x, counts[j], e, value2)
        put_keys(n, t, e, key2)
        sent[jnp.where(j == g + 1, ENTERING, jnp.where(j == g, MIDDLE, UNUSED))] = sent_rows(x)
        query2[jnp.where(j == g + 1, 0, 1)] = make_query(sent_rows(n).reshape(HALF, HEAD_DIM), t)

    def blocks_of(j):
        return list_blocks(lambda i: mask[0, j, i], lambda i: counts[i])

    todo[0] = g + 1
    wanted = jnp.where(g < SPANS - 1, 1, 0)
    todo[wanted] = g
    wanted += 1
    for j in range(1, SPANS):
        todo[wanted] = j
        wanted += jnp.where(jnp.logical_and(j < g, mask[1, g, j - 1] > 0), 1, 0)

    least[...] = jnp.ones((8, HEAD_DIM), jnp.float32)

    def one(m, carry):
        j, before = todo[m], todo[jnp.maximum(m - 1, 0)]
        size = blocks_of(j)
        slot = lax.rem(m, 2)

        def block(rows):
            enter(before, 1 - slot, m > 0)
            attend(query[j, :rows], rows, key, value, size, slot)

        rows = jnp.where(jnp.logical_or(j == g + 1, j == g), SPAN, counts[j])
        for r in range(2, PER_SPAN + 1):
            fits = rows <= r * KEYS
            if r > 2:
                fits = jnp.logical_and(fits, rows > (r - 1) * KEYS)
            pl.when(fits)(functools.partial(block, r * KEYS))
        return carry

    lax.fori_loop(0, wanted, one, 0)
    enter(todo[wanted - 1], lax.rem(wanted - 1, 2))

    @pl.when(jnp.min(least[...]) < SMALL)
    def _():
        def one_safe(m, carry):
            j = todo[m]
            attend_safe(query[j], SPAN, key, value, blocks_of(j), lambda i: counts[i], 0)
            enter(j, 0)
            return carry

        lax.fori_loop(0, wanted, one_safe, 0)

    @pl.when(g == SPANS - 1)
    def _():
        x = fresh[...]
        t = steps[1, g]
        n = normed(x)
        put_values(x, counts[SPANS], SPANS - 1, value2)
        put_keys(n, t, SPANS - 1, key2)
        sent[ENTERING] = sent_rows(x)
        query2[0] = make_query(sent_rows(n).reshape(HALF, HEAD_DIM), t)

    size = list_blocks(lambda e: mask[1, g, e], lambda e: counts[e + 1])
    out[:, :8] = sent[MIDDLE].astype(jnp.bfloat16)
    attend(query2[0], HALF, key2, value2, size, 0)

    def put_final():
        x, total = finish(sent[ENTERING].reshape(HALF, HEAD_DIM), HALF, 0, delta[steps[1, g]])
        out[:, 8:] = x.astype(jnp.float32).reshape(SPAN // 16, 8, HEAD_DIM).astype(jnp.bfloat16)
        return jnp.min(total)

    @pl.when(put_final() < SMALL)
    def _():
        attend_safe(query2[0], HALF, key2, value2, size, lambda e: counts[e + 1], 0)
        put_final()


def mesh_place():
    core = lax.axis_index("core")
    return 2 * lax.axis_index("x") + core, lax.axis_index("half"), lax.axis_index("head"), core


def both_steps(place, counts, steps, mask, delta, q_gain, k_gain, same, other, fresh, interpret=False):
    smem = pl.BlockSpec(memory_space=pltpu.SMEM)
    hbm = pl.BlockSpec(memory_space=pl.ANY)
    vmem = pl.BlockSpec(memory_space=pltpu.VMEM)
    noise_steps = q_gain.shape[0]
    bf16, f32 = jnp.bfloat16, jnp.float32
    return pl.pallas_call(
        functools.partial(head_kernel, place),
        out_shape=jax.ShapeDtypeStruct((SPAN // 16, 16, HEAD_DIM), bf16),
        in_specs=[smem, smem, smem, smem, hbm, hbm, vmem, vmem, vmem],
        out_specs=vmem,
        scratch_shapes=[
            pltpu.VMEM((noise_steps, HEAD_DIM), f32),
            pltpu.VMEM((noise_steps, HEAD_DIM), f32),
            pltpu.VMEM((SPANS, SPAN, HEAD_DIM), bf16),
            pltpu.VMEM((SPANS, SPAN, HEAD_DIM), bf16),
            pltpu.VMEM((NONE + 1, HEAD_DIM, KEYS), bf16),
            pltpu.VMEM((NONE + 1, KEYS, 2 * HEAD_DIM), bf16),
            pltpu.VMEM((2, HALF, HEAD_DIM), bf16),
            pltpu.VMEM((NONE + 1, HEAD_DIM, KEYS), bf16),
            pltpu.VMEM((NONE + 1, KEYS, 2 * HEAD_DIM), bf16),
            pltpu.VMEM((2, SPAN, 2 * HEAD_DIM), f32),
            pltpu.VMEM((SPAN, KEYS), f32),
            pltpu.VMEM((8, HEAD_DIM), f32),
            pltpu.SMEM((NONE + 2 * GROUP,), jnp.int32),
            pltpu.SMEM((SPANS + 2,), jnp.int32),
            pltpu.VMEM((UNUSED + 1, SPAN // 16, 8, HEAD_DIM), f32),
            pltpu.SemaphoreType.DMA((2,)),
        ],
        compiler_params=pltpu.CompilerParams(vmem_limit_bytes=32 * 1024 * 1024),
        interpret=interpret,
    )(counts, steps, mask, delta, q_gain, k_gain, same, other, fresh)


def per_device(latents, new_span, counts, steps, span_mask, q_gain, k_gain, delta):
    rows, width = latents.shape
    heads = width // HEAD_DIM

    def to_heads(block):
        return block.reshape(rows, heads, HEAD_DIM).transpose(1, 0, 2)

    sent = jnp.concatenate([to_heads(latents), to_heads(new_span)], axis=1)
    sent = jnp.broadcast_to(sent[:, None], (heads, 2, 2 * rows, HEAD_DIM)).reshape(2 * heads, 2 * rows, HEAD_DIM)
    got = lax.all_to_all(sent, ("head", "half"), 0, 0, tiled=True)
    mine = got[:, :rows].reshape(SPAN, HEAD_DIM)
    fresh = got[:, rows:].reshape(SPAN, HEAD_DIM)
    same = lax.all_to_all(jnp.broadcast_to(mine, (4, SPAN, HEAD_DIM)), "x", 0, 0, tiled=True)
    other = lax.ppermute(same, "core", [(0, 1), (1, 0)])
    done = both_steps(mesh_place, counts, steps, span_mask, delta, q_gain, k_gain, same, other, fresh)
    back = lax.all_to_all(done, "head", 0, 0, tiled=True)
    return tuple(
        back[:, k * rows : (k + 1) * rows].transpose(1, 0, 2).reshape(rows, width) for k in range(2)
    )


def solution(mesh):
    mesh = Mesh(mesh.devices.reshape(4, 2, 32, 2), ("x", "core", "head", "half"))
    seq = ("head", "half")
    tokens = P(("x", "core", *seq), None)
    in_specs = (tokens, P(seq, None), P(), P(), P(), P(), P(), P())
    return jax.shard_map(per_device, mesh=mesh, in_specs=in_specs, out_specs=(tokens, tokens), check_vma=False)
```

```python
import functools
import math

import jax
import jax.numpy as jnp
from jax import lax
from jax.experimental import pallas as pl
from jax.experimental.pallas import tpu as pltpu
from jax.sharding import Mesh
from jax.sharding import PartitionSpec as P

HEAD_DIM = 128
SPAN = 512
SPANS = 8
HALF = SPAN // 2
KEYS = 128
PER_SPAN = SPAN // KEYS
NONE = SPANS * PER_SPAN
FIRST = (4, 6, 8)
REST = (2, 4, 8)
ENTERING, MIDDLE, UNUSED = 0, 1, 2
SCORE_SCALE = math.log2(math.e) / math.sqrt(HEAD_DIM)
SHIFT = 40.0
SMALL = 2.0**-60


def normed(x):
    x = x.astype(jnp.float32)
    return x * lax.rsqrt(jnp.mean(x * x, axis=-1, keepdims=True) + 1e-06)


def head_kernel(
    place,
    counts,
    steps,
    mask,
    delta,
    q_gain,
    k_gain,
    same,
    other,
    fresh,
    out,
    qg,
    kg,
    xs,
    query,
    key,
    value,
    query2,
    key2,
    value2,
    acc,
    top,
    least,
    blocks,
    todo,
    sent,
    sems,
):
    g, half, head, core = place()
    cols = pl.ds(pl.multiple_of(head * HEAD_DIM, HEAD_DIM), HEAD_DIM)
    copies = [
        pltpu.make_async_copy(q_gain.at[:, cols], qg, sems.at[0]),
        pltpu.make_async_copy(k_gain.at[:, cols], kg, sems.at[1]),
    ]
    for copy in copies:
        copy.start()
    for keys, values in ((key, value), (key2, value2)):
        keys[NONE] = jnp.zeros((HEAD_DIM, KEYS), jnp.bfloat16)
        values[NONE] = jnp.zeros((KEYS, 2 * HEAD_DIM), jnp.bfloat16)

    def put_values(x, live, i, values):
        alive = lax.broadcasted_iota(jnp.int32, (SPAN, HEAD_DIM), 0) < live
        kept = jnp.where(alive, x.astype(jnp.float32), 0.0).astype(jnp.bfloat16)
        ones = jnp.where(alive, 1.0, 0.0).astype(jnp.bfloat16)
        for r in range(PER_SPAN):
            values[PER_SPAN * i + r, :, :HEAD_DIM] = kept[r * KEYS : (r + 1) * KEYS]
            values[PER_SPAN * i + r, :, HEAD_DIM:] = ones[r * KEYS : (r + 1) * KEYS]

    def put_keys(n, t, i, keys):
        turned = (n * kg[pl.ds(t, 1), :]).astype(jnp.bfloat16).T
        for r in range(PER_SPAN):
            keys[PER_SPAN * i + r] = turned[:, r * KEYS : (r + 1) * KEYS]

    def make_query(n, t):
        return (n * qg[pl.ds(t, 1), :]).astype(jnp.bfloat16)

    last = jnp.minimum(g + 1, SPANS - 1)

    def each_pair(step):
        for a in range(SPANS // 2):

            @pl.when(2 * a <= last)
            def _():
                for source, j in ((same, 2 * a + core), (other, 2 * a + 1 - core)):
                    step(source[a], j)

    def values_of(x, j):
        xs[j] = x
        put_values(x, counts[j], j, value)

    def keys_of(x, j):
        t = steps[0, j]
        n = normed(x)
        put_keys(n, t, j, key)
        query[j] = make_query(n, t)

    each_pair(values_of)
    for copy in copies:
        copy.wait()
    each_pair(keys_of)

    def list_blocks(seen, live):
        size = jnp.int32(0)
        for i in range(SPANS):
            for r in range(PER_SPAN):
                blocks[size + r] = PER_SPAN * i + r
            size += jnp.where(seen(i) > 0, (live(i) + KEYS - 1) // KEYS, 0)
        for r in range(2 * FIRST[-1]):
            blocks[size + r] = NONE
        return size

    def group(q, keys, values, first, pairs):
        weights, parts = [], []
        for r in range(pairs):
            left, right = blocks[first + 2 * r], blocks[first + 2 * r + 1]
            score = jnp.dot(
                q, jnp.concatenate([keys[left], keys[right]], axis=1), preferred_element_type=jnp.float32
            )
            weights.append(jnp.exp2(score * SCORE_SCALE - SHIFT).astype(jnp.bfloat16))
        for r in range(pairs):
            left, right = blocks[first + 2 * r], blocks[first + 2 * r + 1]
            parts.append(
                jnp.dot(
                    weights[r],
                    jnp.concatenate([values[left], values[right]], axis=0),
                    preferred_element_type=jnp.float32,
                )
            )
        return sum(parts[1:], parts[0])

    def attend(q, rows, keys, values, size, slot, pairs):
        acc[slot, :rows] = group(q, keys, values, 0, pairs)
        if rows < SPAN:
            acc[slot, rows:] = jnp.ones((SPAN - rows, 2 * HEAD_DIM), jnp.float32)
        if pairs == FIRST[-1]:
            rest = (size + 1) // 2 - pairs
            for least_rest, more in zip((0, *REST), REST):

                @pl.when(jnp.logical_and(rest > least_rest, rest <= more))
                def _():
                    acc[slot, :rows] += group(q, keys, values, 2 * pairs, more)

    def by_size(size, step):
        pairs = (size + 1) // 2
        for fewer, most in zip((0, *FIRST), FIRST):
            fits = pairs > fewer if most == FIRST[-1] else jnp.logical_and(pairs > fewer, pairs <= most)
            pl.when(fits)(functools.partial(step, most))

    def attend_safe(q, rows, keys, values, size, live, slot):
        def scores(b):
            score = jnp.dot(q, keys[b], preferred_element_type=jnp.float32) * SCORE_SCALE
            at = lax.broadcasted_iota(jnp.int32, (rows, KEYS), 1) + lax.rem(b, PER_SPAN) * KEYS
            return jnp.where(at < live(b // PER_SPAN), score, -1e30)

        def highest(n, carry):
            top[:rows] = jnp.maximum(top[:rows], jnp.max(scores(blocks[n]), axis=-1, keepdims=True))
            return carry

        def add(n, carry):
            weight = jnp.exp2(scores(blocks[n]) - top[:rows]).astype(jnp.bfloat16)
            acc[slot, :rows] += jnp.dot(weight, values[blocks[n]], preferred_element_type=jnp.float32)
            return carry

        top[:rows] = jnp.full((rows, KEYS), -1e30, jnp.float32)
        acc[slot, :rows] = jnp.zeros((rows, 2 * HEAD_DIM), jnp.float32)
        lax.fori_loop(0, size, highest, 0)
        lax.fori_loop(0, size, add, 0)

    def finish(x, rows, slot, rate):
        total = acc[slot, :rows, HEAD_DIM:]
        target = (acc[slot, :rows, :HEAD_DIM] / total).astype(jnp.bfloat16).astype(jnp.float32)
        old = x.astype(jnp.float32)
        return (old + rate * (target - old)).astype(jnp.bfloat16), total

    def sent_rows(x):
        pieces = x.astype(jnp.float32).reshape(SPAN // 16, 2, 8, HEAD_DIM)
        return jnp.where(half == 0, pieces[:, 0], pieces[:, 1])

    def enter(j, slot, counted=True):
        x, total = finish(xs[j], SPAN, slot, delta[steps[0, j]])
        smallest = jnp.min(total.reshape(SPAN // 8, 8, HEAD_DIM), axis=0)
        least[...] = jnp.minimum(least[...], jnp.where(counted, smallest, 1.0))
        e = jnp.where(j > 0, j - 1, SPANS - 1)
        t = steps[1, e]
        n = normed(x)
        put_values(x, counts[j], e, value2)
        put_keys(n, t, e, key2)
        sent[jnp.where(j == g + 1, ENTERING, jnp.where(j == g, MIDDLE, UNUSED))] = sent_rows(x)
        query2[jnp.where(j == g + 1, 0, 1)] = make_query(sent_rows(n).reshape(HALF, HEAD_DIM), t)

    def blocks_of(j):
        return list_blocks(lambda i: mask[0, j, i], lambda i: counts[i])

    todo[0] = g + 1
    wanted = jnp.where(g < SPANS - 1, 1, 0)
    todo[wanted] = g
    wanted += 1
    for j in range(1, SPANS):
        todo[wanted] = j
        wanted += jnp.where(jnp.logical_and(j < g, mask[1, g, j - 1] > 0), 1, 0)

    least[...] = jnp.ones((8, HEAD_DIM), jnp.float32)

    def one(m, carry):
        j, before = todo[m], todo[jnp.maximum(m - 1, 0)]
        size = blocks_of(j)
        slot = lax.rem(m, 2)

        def block(rows, pairs):
            enter(before, 1 - slot, m > 0)
            attend(query[j, :rows], rows, key, value, size, slot, pairs)

        rows = jnp.where(jnp.logical_or(j == g + 1, j == g), SPAN, counts[j])
        for r in range(2, PER_SPAN + 1):
            fits = rows <= r * KEYS
            if r > 2:
                fits = jnp.logical_and(fits, rows > (r - 1) * KEYS)
            pl.when(fits)(lambda r=r: by_size(size, functools.partial(block, r * KEYS)))
        return carry

    lax.fori_loop(0, wanted, one, 0)
    enter(todo[wanted - 1], lax.rem(wanted - 1, 2))

    @pl.when(jnp.min(least[...]) < SMALL)
    def _():
        def one_safe(m, carry):
            j = todo[m]
            attend_safe(query[j], SPAN, key, value, blocks_of(j), lambda i: counts[i], 0)
            enter(j, 0)
            return carry

        lax.fori_loop(0, wanted, one_safe, 0)

    @pl.when(g == SPANS - 1)
    def _():
        x = fresh[...]
        t = steps[1, g]
        n = normed(x)
        put_values(x, counts[SPANS], SPANS - 1, value2)
        put_keys(n, t, SPANS - 1, key2)
        sent[ENTERING] = sent_rows(x)
        query2[0] = make_query(sent_rows(n).reshape(HALF, HEAD_DIM), t)

    size = list_blocks(lambda e: mask[1, g, e], lambda e: counts[e + 1])
    out[:, :8] = sent[MIDDLE].astype(jnp.bfloat16)
    by_size(size, lambda pairs: attend(query2[0], HALF, key2, value2, size, 0, pairs))

    def put_final():
        x, total = finish(sent[ENTERING].reshape(HALF, HEAD_DIM), HALF, 0, delta[steps[1, g]])
        out[:, 8:] = x.astype(jnp.float32).reshape(SPAN // 16, 8, HEAD_DIM).astype(jnp.bfloat16)
        return jnp.min(total)

    @pl.when(put_final() < SMALL)
    def _():
        attend_safe(query2[0], HALF, key2, value2, size, lambda e: counts[e + 1], 0)
        put_final()


def mesh_place():
    core = lax.axis_index("core")
    return 2 * lax.axis_index("x") + core, lax.axis_index("half"), lax.axis_index("head"), core


def both_steps(place, counts, steps, mask, delta, q_gain, k_gain, same, other, fresh, interpret=False):
    smem = pl.BlockSpec(memory_space=pltpu.SMEM)
    hbm = pl.BlockSpec(memory_space=pl.ANY)
    vmem = pl.BlockSpec(memory_space=pltpu.VMEM)
    noise_steps = q_gain.shape[0]
    bf16, f32 = jnp.bfloat16, jnp.float32
    return pl.pallas_call(
        functools.partial(head_kernel, place),
        out_shape=jax.ShapeDtypeStruct((SPAN // 16, 16, HEAD_DIM), bf16),
        in_specs=[smem, smem, smem, smem, hbm, hbm, vmem, vmem, vmem],
        out_specs=vmem,
        scratch_shapes=[
            pltpu.VMEM((noise_steps, HEAD_DIM), f32),
            pltpu.VMEM((noise_steps, HEAD_DIM), f32),
            pltpu.VMEM((SPANS, SPAN, HEAD_DIM), bf16),
            pltpu.VMEM((SPANS, SPAN, HEAD_DIM), bf16),
            pltpu.VMEM((NONE + 1, HEAD_DIM, KEYS), bf16),
            pltpu.VMEM((NONE + 1, KEYS, 2 * HEAD_DIM), bf16),
            pltpu.VMEM((2, HALF, HEAD_DIM), bf16),
            pltpu.VMEM((NONE + 1, HEAD_DIM, KEYS), bf16),
            pltpu.VMEM((NONE + 1, KEYS, 2 * HEAD_DIM), bf16),
            pltpu.VMEM((2, SPAN, 2 * HEAD_DIM), f32),
            pltpu.VMEM((SPAN, KEYS), f32),
            pltpu.VMEM((8, HEAD_DIM), f32),
            pltpu.SMEM((NONE + 2 * FIRST[-1],), jnp.int32),
            pltpu.SMEM((SPANS + 2,), jnp.int32),
            pltpu.VMEM((UNUSED + 1, SPAN // 16, 8, HEAD_DIM), f32),
            pltpu.SemaphoreType.DMA((2,)),
        ],
        compiler_params=pltpu.CompilerParams(vmem_limit_bytes=32 * 1024 * 1024),
        interpret=interpret,
    )(counts, steps, mask, delta, q_gain, k_gain, same, other, fresh)


def per_device(latents, new_span, counts, steps, span_mask, q_gain, k_gain, delta):
    rows, width = latents.shape
    heads = width // HEAD_DIM

    def to_heads(block):
        return block.reshape(rows, heads, HEAD_DIM).transpose(1, 0, 2)

    sent = jnp.concatenate([to_heads(latents), to_heads(new_span)], axis=1)
    sent = jnp.broadcast_to(sent[:, None], (heads, 2, 2 * rows, HEAD_DIM)).reshape(2 * heads, 2 * rows, HEAD_DIM)
    got = lax.all_to_all(sent, ("head", "half"), 0, 0, tiled=True)
    mine = got[:, :rows].reshape(SPAN, HEAD_DIM)
    fresh = got[:, rows:].reshape(SPAN, HEAD_DIM)
    same = lax.all_to_all(jnp.broadcast_to(mine, (4, SPAN, HEAD_DIM)), "x", 0, 0, tiled=True)
    other = lax.ppermute(same, "core", [(0, 1), (1, 0)])
    done = both_steps(mesh_place, counts, steps, span_mask, delta, q_gain, k_gain, same, other, fresh)
    back = lax.all_to_all(done, "head", 0, 0, tiled=True)
    return tuple(
        back[:, k * rows : (k + 1) * rows].transpose(1, 0, 2).reshape(rows, width) for k in range(2)
    )


def solution(mesh):
    mesh = Mesh(mesh.devices.reshape(4, 2, 32, 2), ("x", "core", "head", "half"))
    seq = ("head", "half")
    tokens = P(("x", "core", *seq), None)
    in_specs = (tokens, P(seq, None), P(), P(), P(), P(), P(), P())
    return jax.shard_map(per_device, mesh=mesh, in_specs=in_specs, out_specs=(tokens, tokens), check_vma=False)
```

```python
import functools
import math

import jax
import jax.numpy as jnp
from jax import lax
from jax.experimental import pallas as pl
from jax.experimental.pallas import tpu as pltpu
from jax.sharding import Mesh
from jax.sharding import PartitionSpec as P

HEAD_DIM = 128
SPAN = 512
SPANS = 8
HALF = SPAN // 2
KEYS = 128
PER_SPAN = SPAN // KEYS
NONE = SPANS * PER_SPAN
FIRST = (4, 6, 8)
REST = (2, 4, 8)
ENTERING, MIDDLE, UNUSED = 0, 1, 2
SCORE_SCALE = math.log2(math.e) / math.sqrt(HEAD_DIM)
SHIFT = 40.0
SMALL = 2.0**-60


def normed(x):
    x = x.astype(jnp.float32)
    return x * lax.rsqrt(jnp.mean(x * x, axis=-1, keepdims=True) + 1e-06)


def head_kernel(
    place,
    counts,
    steps,
    mask,
    delta,
    q_gain,
    k_gain,
    same,
    other,
    fresh,
    out,
    qg,
    kg,
    xs,
    query,
    key,
    value,
    query2,
    key2,
    value2,
    acc,
    top,
    least,
    blocks,
    todo,
    sent,
    sems,
):
    g, half, head, core = place()
    cols = pl.ds(pl.multiple_of(head * HEAD_DIM, HEAD_DIM), HEAD_DIM)
    copies = [
        pltpu.make_async_copy(q_gain.at[:, cols], qg, sems.at[0]),
        pltpu.make_async_copy(k_gain.at[:, cols], kg, sems.at[1]),
    ]
    for copy in copies:
        copy.start()
    for keys, values in ((key, value), (key2, value2)):
        keys[NONE] = jnp.zeros((HEAD_DIM, KEYS), jnp.bfloat16)
        values[NONE] = jnp.zeros((KEYS, 2 * HEAD_DIM), jnp.bfloat16)

    def put_values(x, live, i, values):
        alive = lax.broadcasted_iota(jnp.int32, (SPAN, HEAD_DIM), 0) < live
        kept = jnp.where(alive, x.astype(jnp.float32), 0.0).astype(jnp.bfloat16)
        ones = jnp.where(alive, 1.0, 0.0).astype(jnp.bfloat16)
        for r in range(PER_SPAN):
            values[PER_SPAN * i + r, :, :HEAD_DIM] = kept[r * KEYS : (r + 1) * KEYS]
            values[PER_SPAN * i + r, :, HEAD_DIM:] = ones[r * KEYS : (r + 1) * KEYS]

    def put_keys(n, t, i, keys):
        turned = (n * kg[pl.ds(t, 1), :]).astype(jnp.bfloat16).T
        for r in range(PER_SPAN):
            keys[PER_SPAN * i + r] = turned[:, r * KEYS : (r + 1) * KEYS]

    def make_query(n, t):
        return (n * qg[pl.ds(t, 1), :]).astype(jnp.bfloat16)

    last = jnp.minimum(g + 1, SPANS - 1)

    def each_pair(step):
        for a in range(SPANS // 2):

            @pl.when(2 * a <= last)
            def _():
                for source, j in ((same, 2 * a + core), (other, 2 * a + 1 - core)):
                    step(source[a], j)

    def values_of(x, j):
        xs[j] = x
        put_values(x, counts[j], j, value)

    def keys_of(x, j):
        t = steps[0, j]
        n = normed(x)
        put_keys(n, t, j, key)
        query[j] = make_query(n, t)

    each_pair(values_of)
    for copy in copies:
        copy.wait()
    each_pair(keys_of)

    def list_blocks(seen, live):
        size = jnp.int32(0)
        for i in range(SPANS):
            for r in range(PER_SPAN):
                blocks[size + r] = PER_SPAN * i + r
            size += jnp.where(seen(i) > 0, (live(i) + KEYS - 1) // KEYS, 0)
        for r in range(2 * FIRST[-1]):
            blocks[size + r] = NONE
        return size

    def group(q, keys, values, first, pairs):
        weights, parts = [], []
        for r in range(pairs):
            left, right = blocks[first + 2 * r], blocks[first + 2 * r + 1]
            score = jnp.dot(
                q, jnp.concatenate([keys[left], keys[right]], axis=1), preferred_element_type=jnp.float32
            )
            weights.append(jnp.exp2(score * SCORE_SCALE - SHIFT).astype(jnp.bfloat16))
        for r in range(pairs):
            left, right = blocks[first + 2 * r], blocks[first + 2 * r + 1]
            parts.append(
                jnp.dot(
                    weights[r],
                    jnp.concatenate([values[left], values[right]], axis=0),
                    preferred_element_type=jnp.float32,
                )
            )
        return sum(parts[1:], parts[0])

    def attend(q, rows, keys, values, size, slot, pairs):
        acc[slot, :rows] = group(q, keys, values, 0, pairs)
        if rows < SPAN:
            acc[slot, rows:] = jnp.ones((SPAN - rows, 2 * HEAD_DIM), jnp.float32)
        if pairs == FIRST[-1]:
            rest = (size + 1) // 2 - pairs
            for least_rest, more in zip((0, *REST), REST):

                @pl.when(jnp.logical_and(rest > least_rest, rest <= more))
                def _():
                    acc[slot, :rows] += group(q, keys, values, 2 * pairs, more)

    def by_size(size, step):
        pairs = (size + 1) // 2
        for fewer, most in zip((0, *FIRST), FIRST):
            fits = pairs > fewer if most == FIRST[-1] else jnp.logical_and(pairs > fewer, pairs <= most)
            pl.when(fits)(functools.partial(step, most))

    def attend_safe(q, rows, keys, values, size, live, slot):
        def scores(b):
            score = jnp.dot(q, keys[b], preferred_element_type=jnp.float32) * SCORE_SCALE
            at = lax.broadcasted_iota(jnp.int32, (rows, KEYS), 1) + lax.rem(b, PER_SPAN) * KEYS
            return jnp.where(at < live(b // PER_SPAN), score, -1e30)

        def highest(n, carry):
            top[:rows] = jnp.maximum(top[:rows], jnp.max(scores(blocks[n]), axis=-1, keepdims=True))
            return carry

        def add(n, carry):
            weight = jnp.exp2(scores(blocks[n]) - top[:rows]).astype(jnp.bfloat16)
            acc[slot, :rows] += jnp.dot(weight, values[blocks[n]], preferred_element_type=jnp.float32)
            return carry

        top[:rows] = jnp.full((rows, KEYS), -1e30, jnp.float32)
        acc[slot, :rows] = jnp.zeros((rows, 2 * HEAD_DIM), jnp.float32)
        lax.fori_loop(0, size, highest, 0)
        lax.fori_loop(0, size, add, 0)

    def finish(x, rows, slot, rate):
        total = acc[slot, :rows, HEAD_DIM:]
        target = (acc[slot, :rows, :HEAD_DIM] / total).astype(jnp.bfloat16).astype(jnp.float32)
        old = x.astype(jnp.float32)
        return (old + rate * (target - old)).astype(jnp.bfloat16), total

    def sent_rows(x):
        x = x.astype(jnp.float32)
        return jnp.where(half == 0, x[:HALF], x[HALF:]).reshape(HALF // 8, 8, HEAD_DIM)

    def enter(j, slot, counted=True):
        x, total = finish(xs[j], SPAN, slot, delta[steps[0, j]])
        smallest = jnp.min(total.reshape(SPAN // 8, 8, HEAD_DIM), axis=0)
        least[...] = jnp.minimum(least[...], jnp.where(counted, smallest, 1.0))
        e = jnp.where(j > 0, j - 1, SPANS - 1)
        t = steps[1, e]
        n = normed(x)
        put_values(x, counts[j], e, value2)
        put_keys(n, t, e, key2)
        sent[jnp.where(j == g + 1, ENTERING, jnp.where(j == g, MIDDLE, UNUSED))] = sent_rows(x)
        query2[jnp.where(j == g + 1, 0, 1)] = make_query(sent_rows(n).reshape(HALF, HEAD_DIM), t)

    def blocks_of(j):
        return list_blocks(lambda i: mask[0, j, i], lambda i: counts[i])

    todo[0] = g + 1
    wanted = jnp.where(g < SPANS - 1, 1, 0)
    todo[wanted] = g
    wanted += 1
    for j in range(1, SPANS):
        todo[wanted] = j
        wanted += jnp.where(jnp.logical_and(j < g, mask[1, g, j - 1] > 0), 1, 0)

    least[...] = jnp.ones((8, HEAD_DIM), jnp.float32)

    def one(m, carry):
        j, before = todo[m], todo[jnp.maximum(m - 1, 0)]
        size = blocks_of(j)
        slot = lax.rem(m, 2)

        def block(rows, pairs):
            enter(before, 1 - slot, m > 0)
            attend(query[j, :rows], rows, key, value, size, slot, pairs)

        rows = jnp.where(jnp.logical_or(j == g + 1, j == g), SPAN, counts[j])
        for r in range(2, PER_SPAN + 1):
            fits = rows <= r * KEYS
            if r > 2:
                fits = jnp.logical_and(fits, rows > (r - 1) * KEYS)
            pl.when(fits)(lambda r=r: by_size(size, functools.partial(block, r * KEYS)))
        return carry

    lax.fori_loop(0, wanted, one, 0)
    enter(todo[wanted - 1], lax.rem(wanted - 1, 2))

    @pl.when(jnp.min(least[...]) < SMALL)
    def _():
        def one_safe(m, carry):
            j = todo[m]
            attend_safe(query[j], SPAN, key, value, blocks_of(j), lambda i: counts[i], 0)
            enter(j, 0)
            return carry

        lax.fori_loop(0, wanted, one_safe, 0)

    @pl.when(g == SPANS - 1)
    def _():
        x = fresh[...]
        t = steps[1, g]
        n = normed(x)
        put_values(x, counts[SPANS], SPANS - 1, value2)
        put_keys(n, t, SPANS - 1, key2)
        sent[ENTERING] = sent_rows(x)
        query2[0] = make_query(sent_rows(n).reshape(HALF, HEAD_DIM), t)

    size = list_blocks(lambda e: mask[1, g, e], lambda e: counts[e + 1])
    out[:, :8] = sent[MIDDLE].astype(jnp.bfloat16)
    by_size(size, lambda pairs: attend(query2[0], HALF, key2, value2, size, 0, pairs))

    def put_final():
        x, total = finish(sent[ENTERING].reshape(HALF, HEAD_DIM), HALF, 0, delta[steps[1, g]])
        out[:, 8:] = x.astype(jnp.float32).reshape(SPAN // 16, 8, HEAD_DIM).astype(jnp.bfloat16)
        return jnp.min(total)

    @pl.when(put_final() < SMALL)
    def _():
        attend_safe(query2[0], HALF, key2, value2, size, lambda e: counts[e + 1], 0)
        put_final()


def mesh_place():
    core = lax.axis_index("core")
    return 2 * lax.axis_index("x") + core, lax.axis_index("half"), lax.axis_index("head"), core


def both_steps(place, counts, steps, mask, delta, q_gain, k_gain, same, other, fresh, interpret=False):
    smem = pl.BlockSpec(memory_space=pltpu.SMEM)
    hbm = pl.BlockSpec(memory_space=pl.ANY)
    vmem = pl.BlockSpec(memory_space=pltpu.VMEM)
    noise_steps = q_gain.shape[0]
    bf16, f32 = jnp.bfloat16, jnp.float32
    return pl.pallas_call(
        functools.partial(head_kernel, place),
        out_shape=jax.ShapeDtypeStruct((SPAN // 16, 16, HEAD_DIM), bf16),
        in_specs=[smem, smem, smem, smem, hbm, hbm, vmem, vmem, vmem],
        out_specs=vmem,
        scratch_shapes=[
            pltpu.VMEM((noise_steps, HEAD_DIM), f32),
            pltpu.VMEM((noise_steps, HEAD_DIM), f32),
            pltpu.VMEM((SPANS, SPAN, HEAD_DIM), bf16),
            pltpu.VMEM((SPANS, SPAN, HEAD_DIM), bf16),
            pltpu.VMEM((NONE + 1, HEAD_DIM, KEYS), bf16),
            pltpu.VMEM((NONE + 1, KEYS, 2 * HEAD_DIM), bf16),
            pltpu.VMEM((2, HALF, HEAD_DIM), bf16),
            pltpu.VMEM((NONE + 1, HEAD_DIM, KEYS), bf16),
            pltpu.VMEM((NONE + 1, KEYS, 2 * HEAD_DIM), bf16),
            pltpu.VMEM((2, SPAN, 2 * HEAD_DIM), f32),
            pltpu.VMEM((SPAN, KEYS), f32),
            pltpu.VMEM((8, HEAD_DIM), f32),
            pltpu.SMEM((NONE + 2 * FIRST[-1],), jnp.int32),
            pltpu.SMEM((SPANS + 2,), jnp.int32),
            pltpu.VMEM((UNUSED + 1, SPAN // 16, 8, HEAD_DIM), f32),
            pltpu.SemaphoreType.DMA((2,)),
        ],
        compiler_params=pltpu.CompilerParams(vmem_limit_bytes=32 * 1024 * 1024),
        interpret=interpret,
    )(counts, steps, mask, delta, q_gain, k_gain, same, other, fresh)


def per_device(latents, new_span, counts, steps, span_mask, q_gain, k_gain, delta):
    rows, width = latents.shape
    heads = width // HEAD_DIM

    def to_heads(block):
        return block.reshape(rows, heads, HEAD_DIM).transpose(1, 0, 2)

    sent = jnp.concatenate([to_heads(latents), to_heads(new_span)], axis=1)
    sent = jnp.broadcast_to(sent, (2, heads, 2 * rows, HEAD_DIM)).reshape(2 * heads, 2 * rows, HEAD_DIM)
    got = lax.all_to_all(sent, ("half", "head"), 0, 0, tiled=True)
    mine = got[:, :rows].reshape(SPAN, HEAD_DIM)
    fresh = got[:, rows:].reshape(SPAN, HEAD_DIM)
    same = lax.all_to_all(jnp.broadcast_to(mine, (4, SPAN, HEAD_DIM)), "x", 0, 0, tiled=True)
    other = lax.ppermute(same, "core", [(0, 1), (1, 0)])
    done = both_steps(mesh_place, counts, steps, span_mask, delta, q_gain, k_gain, same, other, fresh)
    back = lax.all_to_all(done, "head", 0, 0, tiled=True)
    return tuple(
        back[:, k * rows : (k + 1) * rows].transpose(1, 0, 2).reshape(rows, width) for k in range(2)
    )


def solution(mesh):
    mesh = Mesh(mesh.devices.reshape(4, 2, 2, 32), ("x", "core", "half", "head"))
    seq = ("half", "head")
    tokens = P(("x", "core", *seq), None)
    in_specs = (tokens, P(seq, None), P(), P(), P(), P(), P(), P())
    return jax.shard_map(per_device, mesh=mesh, in_specs=in_specs, out_specs=(tokens, tokens), check_vma=False)
```

```python
import functools
import math

import jax
import jax.numpy as jnp
from jax import lax
from jax.experimental import pallas as pl
from jax.experimental.pallas import tpu as pltpu
from jax.sharding import Mesh
from jax.sharding import PartitionSpec as P

HEAD_DIM = 128
SPAN = 512
SPANS = 8
HALF = SPAN // 2
KEYS = 128
PER_SPAN = SPAN // KEYS
NONE = SPANS * PER_SPAN
FIRST = (4, 6, 8)
REST = (2, 4, 8)
ENTERING, MIDDLE, UNUSED = 0, 1, 2
SCORE_SCALE = math.log2(math.e) / math.sqrt(HEAD_DIM)
SHIFT = 40.0
SMALL = 2.0**-60


def normed(x):
    x = x.astype(jnp.float32)
    return x * lax.rsqrt(jnp.mean(x * x, axis=-1, keepdims=True) + 1e-06)


def head_kernel(
    place,
    counts,
    steps,
    mask,
    delta,
    q_gain,
    k_gain,
    same,
    other,
    fresh,
    out,
    qg,
    kg,
    xs,
    query,
    key,
    value,
    query2,
    key2,
    value2,
    acc,
    top,
    least,
    blocks,
    todo,
    sent,
    sems,
):
    g, half, head, core = place()
    cols = pl.ds(pl.multiple_of(head * HEAD_DIM, HEAD_DIM), HEAD_DIM)
    copies = [
        pltpu.make_async_copy(q_gain.at[:, cols], qg, sems.at[0]),
        pltpu.make_async_copy(k_gain.at[:, cols], kg, sems.at[1]),
    ]
    for copy in copies:
        copy.start()
    for keys, values in ((key, value), (key2, value2)):
        keys[NONE] = jnp.zeros((HEAD_DIM, KEYS), jnp.bfloat16)
        values[NONE] = jnp.zeros((KEYS, 2 * HEAD_DIM), jnp.bfloat16)

    def put_values(x, live, i, values):
        alive = lax.broadcasted_iota(jnp.int32, (SPAN, HEAD_DIM), 0) < live
        kept = jnp.where(alive, x.astype(jnp.float32), 0.0).astype(jnp.bfloat16)
        ones = jnp.where(alive, 1.0, 0.0).astype(jnp.bfloat16)
        for r in range(PER_SPAN):
            values[PER_SPAN * i + r, :, :HEAD_DIM] = kept[r * KEYS : (r + 1) * KEYS]
            values[PER_SPAN * i + r, :, HEAD_DIM:] = ones[r * KEYS : (r + 1) * KEYS]

    def put_keys(n, t, i, keys):
        turned = (n * kg[pl.ds(t, 1), :]).astype(jnp.bfloat16).T
        for r in range(PER_SPAN):
            keys[PER_SPAN * i + r] = turned[:, r * KEYS : (r + 1) * KEYS]

    def make_query(n, t):
        return (n * qg[pl.ds(t, 1), :]).astype(jnp.bfloat16)

    last = jnp.minimum(g + 1, SPANS - 1)

    def each_pair(step):
        for a in range(SPANS // 2):

            @pl.when(2 * a <= last)
            def _():
                for source, j in ((same, 2 * a + core), (other, 2 * a + 1 - core)):
                    step(source[a], j)

    def values_of(x, j):
        xs[j] = x
        put_values(x, counts[j], j, value)

    def keys_of(x, j):
        t = steps[0, j]
        n = normed(x)
        put_keys(n, t, j, key)
        query[j] = make_query(n, t)

    each_pair(values_of)
    for copy in copies:
        copy.wait()
    each_pair(keys_of)

    def list_blocks(seen, live):
        size = jnp.int32(0)
        for i in range(SPANS):
            for r in range(PER_SPAN):
                blocks[size + r] = PER_SPAN * i + r
            size += jnp.where(seen(i) > 0, (live(i) + KEYS - 1) // KEYS, 0)
        for r in range(2 * FIRST[-1]):
            blocks[size + r] = NONE
        return size

    def group(q, keys, values, first, pairs):
        weights, parts = [], []
        for r in range(pairs):
            left, right = blocks[first + 2 * r], blocks[first + 2 * r + 1]
            score = jnp.dot(
                q, jnp.concatenate([keys[left], keys[right]], axis=1), preferred_element_type=jnp.float32
            )
            weights.append(jnp.exp2(score * SCORE_SCALE - SHIFT).astype(jnp.bfloat16))
        for r in range(pairs):
            left, right = blocks[first + 2 * r], blocks[first + 2 * r + 1]
            parts.append(
                jnp.dot(
                    weights[r],
                    jnp.concatenate([values[left], values[right]], axis=0),
                    preferred_element_type=jnp.float32,
                )
            )
        return sum(parts[1:], parts[0])

    def attend(q, rows, keys, values, size, slot, pairs):
        acc[slot, :rows] = group(q, keys, values, 0, pairs)
        if rows < SPAN:
            acc[slot, rows:] = jnp.ones((SPAN - rows, 2 * HEAD_DIM), jnp.float32)
        if pairs == FIRST[-1]:
            rest = (size + 1) // 2 - pairs
            for least_rest, more in zip((0, *REST), REST):

                @pl.when(jnp.logical_and(rest > least_rest, rest <= more))
                def _():
                    acc[slot, :rows] += group(q, keys, values, 2 * pairs, more)

    def by_size(size, step):
        pairs = (size + 1) // 2
        for fewer, most in zip((0, *FIRST), FIRST):
            fits = pairs > fewer if most == FIRST[-1] else jnp.logical_and(pairs > fewer, pairs <= most)
            pl.when(fits)(functools.partial(step, most))

    def attend_safe(q, rows, keys, values, size, live, slot):
        def scores(b):
            score = jnp.dot(q, keys[b], preferred_element_type=jnp.float32) * SCORE_SCALE
            at = lax.broadcasted_iota(jnp.int32, (rows, KEYS), 1) + lax.rem(b, PER_SPAN) * KEYS
            return jnp.where(at < live(b // PER_SPAN), score, -1e30)

        def highest(n, carry):
            top[:rows] = jnp.maximum(top[:rows], jnp.max(scores(blocks[n]), axis=-1, keepdims=True))
            return carry

        def add(n, carry):
            weight = jnp.exp2(scores(blocks[n]) - top[:rows]).astype(jnp.bfloat16)
            acc[slot, :rows] += jnp.dot(weight, values[blocks[n]], preferred_element_type=jnp.float32)
            return carry

        top[:rows] = jnp.full((rows, KEYS), -1e30, jnp.float32)
        acc[slot, :rows] = jnp.zeros((rows, 2 * HEAD_DIM), jnp.float32)
        lax.fori_loop(0, size, highest, 0)
        lax.fori_loop(0, size, add, 0)

    def finish(x, rows, slot, rate):
        total = acc[slot, :rows, HEAD_DIM:]
        target = (acc[slot, :rows, :HEAD_DIM] / total).astype(jnp.bfloat16).astype(jnp.float32)
        old = x.astype(jnp.float32)
        return (old + rate * (target - old)).astype(jnp.bfloat16), total

    def sent_rows(x):
        x = x.astype(jnp.float32)
        return jnp.where(half == 0, x[:HALF], x[HALF:]).reshape(HALF // 8, 8, HEAD_DIM)

    def enter(j, slot, counted=True):
        x, total = finish(xs[j], SPAN, slot, delta[steps[0, j]])
        smallest = jnp.min(total.reshape(SPAN // 8, 8, HEAD_DIM), axis=0)
        least[...] = jnp.minimum(least[...], jnp.where(counted, smallest, 1.0))
        e = jnp.where(j > 0, j - 1, SPANS - 1)
        t = steps[1, e]
        n = normed(x)
        put_values(x, counts[j], e, value2)
        put_keys(n, t, e, key2)
        sent[jnp.where(j == g + 1, ENTERING, jnp.where(j == g, MIDDLE, UNUSED))] = sent_rows(x)
        query2[jnp.where(j == g + 1, 0, 1)] = make_query(sent_rows(n).reshape(HALF, HEAD_DIM), t)

    def blocks_of(j):
        return list_blocks(lambda i: mask[0, j, i], lambda i: counts[i])

    todo[0] = g + 1
    wanted = jnp.where(g < SPANS - 1, 1, 0)
    todo[wanted] = g
    wanted += 1
    for j in range(1, SPANS):
        todo[wanted] = j
        wanted += jnp.where(jnp.logical_and(j < g, mask[1, g, j - 1] > 0), 1, 0)

    least[...] = jnp.ones((8, HEAD_DIM), jnp.float32)

    def one(m, carry):
        j, before = todo[m], todo[jnp.maximum(m - 1, 0)]
        size = blocks_of(j)
        slot = lax.rem(m, 2)

        def block(rows, pairs):
            enter(before, 1 - slot, m > 0)
            attend(query[j, :rows], rows, key, value, size, slot, pairs)

        whole = jnp.logical_and(half == 1, jnp.logical_or(j == g + 1, j == g))
        rows = jnp.where(whole, SPAN, counts[j])
        for r in range(2, PER_SPAN + 1):
            fits = rows <= r * KEYS
            if r > 2:
                fits = jnp.logical_and(fits, rows > (r - 1) * KEYS)
            pl.when(fits)(lambda r=r: by_size(size, functools.partial(block, r * KEYS)))
        return carry

    lax.fori_loop(0, wanted, one, 0)
    enter(todo[wanted - 1], lax.rem(wanted - 1, 2))

    @pl.when(jnp.min(least[...]) < SMALL)
    def _():
        def one_safe(m, carry):
            j = todo[m]
            attend_safe(query[j], SPAN, key, value, blocks_of(j), lambda i: counts[i], 0)
            enter(j, 0)
            return carry

        lax.fori_loop(0, wanted, one_safe, 0)

    @pl.when(g == SPANS - 1)
    def _():
        x = fresh[...]
        t = steps[1, g]
        n = normed(x)
        put_values(x, counts[SPANS], SPANS - 1, value2)
        put_keys(n, t, SPANS - 1, key2)
        sent[ENTERING] = sent_rows(x)
        query2[0] = make_query(sent_rows(n).reshape(HALF, HEAD_DIM), t)

    size = list_blocks(lambda e: mask[1, g, e], lambda e: counts[e + 1])
    out[:, :8] = sent[MIDDLE].astype(jnp.bfloat16)
    by_size(size, lambda pairs: attend(query2[0], HALF, key2, value2, size, 0, pairs))

    def put_final():
        x, total = finish(sent[ENTERING].reshape(HALF, HEAD_DIM), HALF, 0, delta[steps[1, g]])
        out[:, 8:] = x.astype(jnp.float32).reshape(SPAN // 16, 8, HEAD_DIM).astype(jnp.bfloat16)
        return jnp.min(total)

    @pl.when(put_final() < SMALL)
    def _():
        attend_safe(query2[0], HALF, key2, value2, size, lambda e: counts[e + 1], 0)
        put_final()


def mesh_place():
    core = lax.axis_index("core")
    return 2 * lax.axis_index("x") + core, lax.axis_index("half"), lax.axis_index("head"), core


def both_steps(place, counts, steps, mask, delta, q_gain, k_gain, same, other, fresh, interpret=False):
    smem = pl.BlockSpec(memory_space=pltpu.SMEM)
    hbm = pl.BlockSpec(memory_space=pl.ANY)
    vmem = pl.BlockSpec(memory_space=pltpu.VMEM)
    noise_steps = q_gain.shape[0]
    bf16, f32 = jnp.bfloat16, jnp.float32
    return pl.pallas_call(
        functools.partial(head_kernel, place),
        out_shape=jax.ShapeDtypeStruct((SPAN // 16, 16, HEAD_DIM), bf16),
        in_specs=[smem, smem, smem, smem, hbm, hbm, vmem, vmem, vmem],
        out_specs=vmem,
        scratch_shapes=[
            pltpu.VMEM((noise_steps, HEAD_DIM), f32),
            pltpu.VMEM((noise_steps, HEAD_DIM), f32),
            pltpu.VMEM((SPANS, SPAN, HEAD_DIM), bf16),
            pltpu.VMEM((SPANS, SPAN, HEAD_DIM), bf16),
            pltpu.VMEM((NONE + 1, HEAD_DIM, KEYS), bf16),
            pltpu.VMEM((NONE + 1, KEYS, 2 * HEAD_DIM), bf16),
            pltpu.VMEM((2, HALF, HEAD_DIM), bf16),
            pltpu.VMEM((NONE + 1, HEAD_DIM, KEYS), bf16),
            pltpu.VMEM((NONE + 1, KEYS, 2 * HEAD_DIM), bf16),
            pltpu.VMEM((2, SPAN, 2 * HEAD_DIM), f32),
            pltpu.VMEM((SPAN, KEYS), f32),
            pltpu.VMEM((8, HEAD_DIM), f32),
            pltpu.SMEM((NONE + 2 * FIRST[-1],), jnp.int32),
            pltpu.SMEM((SPANS + 2,), jnp.int32),
            pltpu.VMEM((UNUSED + 1, SPAN // 16, 8, HEAD_DIM), f32),
            pltpu.SemaphoreType.DMA((2,)),
        ],
        compiler_params=pltpu.CompilerParams(vmem_limit_bytes=32 * 1024 * 1024),
        interpret=interpret,
    )(counts, steps, mask, delta, q_gain, k_gain, same, other, fresh)


def per_device(latents, new_span, counts, steps, span_mask, q_gain, k_gain, delta):
    rows, width = latents.shape
    heads = width // HEAD_DIM

    def to_heads(block):
        return block.reshape(rows, heads, HEAD_DIM).transpose(1, 0, 2)

    sent = jnp.concatenate([to_heads(latents), to_heads(new_span)], axis=1)
    sent = jnp.broadcast_to(sent, (2, heads, 2 * rows, HEAD_DIM)).reshape(2 * heads, 2 * rows, HEAD_DIM)
    got = lax.all_to_all(sent, ("half", "head"), 0, 0, tiled=True)
    mine = got[:, :rows].reshape(SPAN, HEAD_DIM)
    fresh = got[:, rows:].reshape(SPAN, HEAD_DIM)
    same = lax.all_to_all(jnp.broadcast_to(mine, (4, SPAN, HEAD_DIM)), "x", 0, 0, tiled=True)
    other = lax.ppermute(same, "core", [(0, 1), (1, 0)])
    done = both_steps(mesh_place, counts, steps, span_mask, delta, q_gain, k_gain, same, other, fresh)
    back = lax.all_to_all(done, "head", 0, 0, tiled=True)
    return tuple(
        back[:, k * rows : (k + 1) * rows].transpose(1, 0, 2).reshape(rows, width) for k in range(2)
    )


def solution(mesh):
    mesh = Mesh(mesh.devices.reshape(4, 2, 2, 32), ("x", "core", "half", "head"))
    seq = ("half", "head")
    tokens = P(("x", "core", *seq), None)
    in_specs = (tokens, P(seq, None), P(), P(), P(), P(), P(), P())
    return jax.shard_map(per_device, mesh=mesh, in_specs=in_specs, out_specs=(tokens, tokens), check_vma=False)
```
